128 devices in a mesh: batch: 128 (over y, x, z, core).
Axes of the slice: x: 4, y: 4, z: 4, core: 2. Of those that a mesh axis runs over, the one named last changes fastest.
Arguments:
- features: bfloat16 [128, 16, 8, 16, 256], P('batch'), may hold values from -6 to 6
- timesteps: int32 [1024], replicated, may hold values from 0 to 255
- embedding: float32 [256, 1024], replicated, may hold values from -6 to 6
- first_gain: float32 [256], replicated, may hold values from 0.1 to 1.9
- first_shift: float32 [256], replicated, may hold values from -3 to 3
- first_kernel: bfloat16 [3, 3, 256, 256], replicated, may hold values from -0.125 to 0.125
- first_bias: float32 [256], replicated, may hold values from -3 to 3
- time_dense: bfloat16 [1024, 256], replicated, may hold values from -0.1875 to 0.1875
- second_gain: float32 [256], replicated, may hold values from 0.1 to 1.9
- second_shift: float32 [256], replicated, may hold values from -3 to 3
- second_kernel: bfloat16 [3, 3, 256, 256], replicated, may hold values from -0.125 to 0.125
- second_bias: float32 [256], replicated, may hold values from -3 to 3
- mixer_gain: float32 [256], replicated, may hold values from 0.1 to 1.9
- mixer_shift: float32 [256], replicated, may hold values from -3 to 3
- project_in: bfloat16 [256, 768], replicated, may hold values from -0.375 to 0.375
- query_bias: float32 [256], replicated, may hold values from -2 to 2
- value_bias: float32 [256], replicated, may hold values from -2 to 2
- project_out: bfloat16 [256, 256], replicated, may hold values from -1.5 to 1.5
- output_bias: float32 [256], replicated, may hold values from -3 to 3
- cotangent: bfloat16 [128, 16, 8, 16, 256], P('batch'), may hold values from -6 to 6
Outputs:
- result: bfloat16 [128, 16, 8, 16, 256], P('batch')
- input_grad: float32 [128, 16, 8, 16, 256], P('batch')
- embedding_grad: float32 [256, 1024], replicated
- first_gain_grad: float32 [256], replicated
- first_shift_grad: float32 [256], replicated
- first_kernel_grad: float32 [3, 3, 256, 256], replicated
- first_bias_grad: float32 [256], replicated
- time_dense_grad: float32 [1024, 256], replicated
- second_gain_grad: float32 [256], replicated
- second_shift_grad: float32 [256], replicated
- second_kernel_grad: float32 [3, 3, 256, 256], replicated
- second_bias_grad: float32 [256], replicated
- mixer_gain_grad: float32 [256], replicated
- mixer_shift_grad: float32 [256], replicated
- project_in_grad: float32 [256, 768], replicated
- query_bias_grad: float32 [256], replicated
- value_bias_grad: float32 [256], replicated
- project_out_grad: float32 [256, 256], replicated
- output_bias_grad: float32 [256], replicated
The draws below stay inside these ranges and needn't reach their ends.
All inputs are finite; a program needn't handle non-finite values.
Results may differ from the reference program's by a relative error of at most 0.017.
Values may be sent and summed in bfloat16 or wider, within the bound.
No kernel may reach another device: no remote copies, remote signals or barrier semaphores. Data moves between devices by JAX's collectives and lax.ppermute only.
A program may use at most 128 MiB of HBM per device.

```python
import jax
import jax.numpy as jnp
from jax import lax

C = 256
TEMB = 1024
GROUPS = 32
SIDE = 16
STEPS = 256
MAPS_PAIR = 16
HALF = 8
MAPS = 1024
N_BATCH = 128


def set_ends(result, stream_key, low, high):
    place = [jax.random.randint(jax.random.fold_in(stream_key, axis), (), 0, length) for axis, length in enumerate(result.shape)]
    main_axis = result.shape.index(max(result.shape))
    neighbour = place[:main_axis] + [(place[main_axis] + 1) % result.shape[main_axis]] + place[main_axis + 1:]
    return result.at[tuple(place)].set(low).at[tuple(neighbour)].set(high)


def block_scale(own_key, dims, pieces, smallest, top_value):
    def one(position, parts):
        draws = jax.random.uniform(jax.random.fold_in(jax.random.fold_in(own_key, 6), position), (parts,), jnp.float32, smallest / len(pieces), top_value / len(pieces))
        return jnp.repeat(jnp.exp(draws), dims[position] // parts).reshape((-1,) + (1,) * (len(dims) - position - 1))

    level = one(*pieces[0])
    for cut in pieces[1:]:
        level = level * one(*cut)
    return level


def noise(rng, shape, scale, limit, split=(), kind=jnp.bfloat16):
    level = block_scale(rng, shape, split, -0.22, 0.18) if split else 1.0
    values = jax.random.normal(rng, shape, jnp.float32) * scale * level
    return jnp.minimum(jnp.maximum(values, -limit), limit).astype(kind)


def setup_inputs(seed: int = 0) -> dict:
    key_of = jax.random.split(jax.random.key(seed), 21)
    features = noise(key_of[0], (N_BATCH, MAPS_PAIR, HALF, SIDE, C), 1.0, 6.0, ((0, 128),))
    timesteps = set_ends(jax.random.randint(key_of[1], (MAPS,), 0, STEPS), jax.random.fold_in(key_of[1], 1), 0, STEPS - 1).astype(jnp.int32)
    embedding = noise(key_of[2], (STEPS, TEMB), 1.0, 6.0, (), jnp.float32)
    first_gain = jnp.clip(1.0 + 0.18 * jax.random.normal(key_of[3], (C,), jnp.float32), 0.1, 1.9)
    first_shift = noise(key_of[4], (C,), 0.5, 3.0, (), jnp.float32)
    first_kernel = noise(key_of[5], (3, 3, C, C), (9 * C) ** -0.5, 0.125)
    first_bias = noise(key_of[6], (C,), 0.5, 3.0, (), jnp.float32)
    time_dense = noise(key_of[7], (TEMB, C), TEMB ** -0.5, 0.1875)
    second_gain = jnp.clip(1.0 + 0.18 * jax.random.normal(key_of[8], (C,), jnp.float32), 0.1, 1.9)
    second_shift = noise(key_of[9], (C,), 0.5, 3.0, (), jnp.float32)
    second_kernel = noise(key_of[10], (3, 3, C, C), (9 * C) ** -0.5, 0.125)
    second_bias = noise(key_of[11], (C,), 0.5, 3.0, (), jnp.float32)
    mixer_gain = jnp.clip(1.0 + 0.18 * jax.random.normal(key_of[12], (C,), jnp.float32), 0.1, 1.9)
    mixer_shift = noise(key_of[13], (C,), 0.5, 3.0, (), jnp.float32)
    project_in = noise(key_of[14], (C, 3 * C), C ** -0.5, 0.375)
    query_bias = noise(key_of[15], (C,), 0.3, 2.0, (), jnp.float32)
    value_bias = noise(key_of[16], (C,), 0.3, 2.0, (), jnp.float32)
    project_out = noise(key_of[17], (C, C), (C // 16) ** -0.5, 1.5)
    output_bias = noise(key_of[18], (C,), 0.5, 3.0, (), jnp.float32)
    cotangent = noise(key_of[19], (N_BATCH, MAPS_PAIR, HALF, SIDE, C), 1.0, 6.0, ((0, 128),))
    return dict(features=features, timesteps=timesteps, embedding=embedding, first_gain=first_gain, first_shift=first_shift, first_kernel=first_kernel, first_bias=first_bias, time_dense=time_dense, second_gain=second_gain, second_shift=second_shift, second_kernel=second_kernel, second_bias=second_bias, mixer_gain=mixer_gain, mixer_shift=mixer_shift, project_in=project_in, query_bias=query_bias, value_bias=value_bias, project_out=project_out, output_bias=output_bias, cotangent=cotangent)


@jax.custom_vjp
def low(v):
    return lax.optimization_barrier(v.astype(jnp.bfloat16)).astype(jnp.float32)

@jax.custom_vjp
def low_back(v):
    return v

def low_keep(v):
    return (low(v), None)

def low_pass(kept, grad):
    return (grad,)

def back_keep(v):
    return (v, None)

def back_low(kept, grad):
    return (low(grad),)
low.defvjp(low_keep, low_pass)
low_back.defvjp(back_keep, back_low)
HIGHEST = lax.Precision.HIGHEST

def group_norm(values, gain, shift):
    count, rows, cols, channels = values.shape
    grouped = values.reshape(count, rows * cols, GROUPS, channels // GROUPS)
    center = lax.optimization_barrier(jnp.mean(grouped, axis=(1, 3), keepdims=True))
    spread = lax.optimization_barrier(jnp.mean(grouped * grouped, axis=(1, 3), keepdims=True)) - center * center
    normed = (grouped - center) * lax.rsqrt(spread + 1e-05)
    return normed.reshape(values.shape) * gain + shift

def convolve(values, kernel):
    return lax.conv_general_dilated(values, kernel, (1, 1), 'SAME', dimension_numbers=('NHWC', 'HWIO', 'NHWC'), precision=HIGHEST)

def forward(values, onehot, embedding, first_gain, first_shift, first_kernel, first_bias, time_dense, second_gain, second_shift, second_kernel, second_bias, mixer_gain, mixer_shift, project_in, query_bias, value_bias, project_out, output_bias):
    count = values.shape[0]
    channels = values.shape[3]
    active = low(jax.nn.silu(group_norm(values, first_gain, first_shift)))
    time_rows = low(jax.nn.silu(jnp.dot(onehot, embedding, precision=HIGHEST)))
    time_added = jnp.dot(time_rows, time_dense, precision=HIGHEST)
    hidden = low_back(convolve(active, first_kernel) + first_bias + time_added[:, None, None, :])
    second = low(jax.nn.silu(group_norm(hidden, second_gain, second_shift)))
    residual = values + low_back(convolve(second, second_kernel) + second_bias)
    normed = low(group_norm(residual, mixer_gain, mixer_shift)).reshape(count, SIDE * SIDE, channels)
    joined = jnp.einsum('gpc,cd->gpd', normed, project_in, precision=HIGHEST)
    query = low_back(low(joined[..., :channels] + query_bias))
    keys = low_back(low(joined[..., channels:2 * channels]))
    vals = low_back(low(joined[..., 2 * channels:] + value_bias))
    scores = low_back(jnp.einsum('gqc,gkc->gqk', query, keys, precision=HIGHEST) * channels ** (-0.5))
    weights = low(jax.nn.softmax(scores, axis=-1))
    mixed = low_back(low(jnp.einsum('gqk,gkc->gqc', weights, vals, precision=HIGHEST)))
    branch = jnp.einsum('gqc,cd->gqd', mixed, project_out, precision=HIGHEST) + output_bias
    return residual + branch.reshape(count, SIDE, SIDE, channels)

def reference(features, timesteps, embedding, first_gain, first_shift, first_kernel, first_bias, time_dense, second_gain, second_shift, second_kernel, second_bias, mixer_gain, mixer_shift, project_in, query_bias, value_bias, project_out, output_bias, cotangent):
    pairs = N_BATCH // 2

    def to_maps(array):
        shaped = array.astype(jnp.float32).reshape(pairs, 2, MAPS_PAIR, HALF, SIDE, C)
        return shaped.transpose(0, 2, 1, 3, 4, 5).reshape(pairs, MAPS_PAIR, SIDE, SIDE, C)

    def from_maps(array):
        shaped = array.reshape(pairs, MAPS_PAIR, 2, HALF, SIDE, C)
        return shaped.transpose(0, 2, 1, 3, 4, 5).reshape(N_BATCH, MAPS_PAIR, HALF, SIDE, C)
    params = tuple((p.astype(jnp.float32) for p in (embedding, first_gain, first_shift, first_kernel, first_bias, time_dense, second_gain, second_shift, second_kernel, second_bias, mixer_gain, mixer_shift, project_in, query_bias, value_bias, project_out, output_bias)))
    stepped = timesteps.astype(jnp.int32).reshape(pairs, MAPS_PAIR)

    def one_pair(carry, item):
        values, upstream, steps = item
        onehot = (steps[:, None] == jnp.arange(STEPS, dtype=jnp.int32)[None, :]).astype(jnp.float32)
        output, pull = jax.vjp(lambda inputs, *weights: forward(inputs, onehot, *weights), values, *params)
        grads = pull(upstream)
        carry = tuple((total + grad for total, grad in zip(carry, grads[1:])))
        return (carry, (output, grads[0]))
    start = tuple((jnp.zeros_like(p) for p in params))
    totals, (outputs, input_grads) = lax.scan(one_pair, start, (to_maps(features), to_maps(cotangent), stepped))
    return (from_maps(outputs).astype(jnp.bfloat16), from_maps(input_grads), totals[0], totals[1], totals[2], totals[3], totals[4], totals[5], totals[6], totals[7], totals[8], totals[9], totals[10], totals[11], totals[12], totals[13], totals[14], totals[15], totals[16])
```

```python
import jax
import jax.numpy as jnp
from jax import lax
from jax.experimental import pallas as pl
from jax.experimental.pallas import tpu as pltpu
from jax.sharding import PartitionSpec as P

BF = jnp.bfloat16
F32 = jnp.float32
C = 256
SIDE = 16
POS = 256
GROUPS = 32
LANES = 128
EPSILON = 1e-05
OWN = 8
PAD = POS + 2 * SIDE
COUNT = float(POS * C // GROUPS)

G1, S1, B1, G2, S2, B2, G3, S3, BQ, BV, BO = range(11)
MU1, RS1, MU2, RS2 = range(4)


def mm(a, b):
    return jnp.dot(a, b, preferred_element_type=F32)


def mm_nt(a, b):
    return lax.dot_general(a, b, (((1,), (1,)), ((), ())), preferred_element_type=F32)


def mm_tn(a, b):
    return lax.dot_general(a, b, (((0,), (0,)), ((), ())), preferred_element_type=F32)


def group_total(s):
    lane = lax.broadcasted_iota(jnp.int32, s.shape, 1)
    for bit in (1, 2, 4):
        s = s + jnp.where((lane & bit) == 0, pltpu.roll(s, C - bit, 1), pltpu.roll(s, bit, 1))
    return s


def statistics(total, squares):
    mu = group_total(total) * (1.0 / COUNT)
    var = group_total(squares) * (1.0 / COUNT) - mu * mu
    return mu, lax.rsqrt(var + EPSILON)


def logistic(z):
    return 0.5 * jnp.tanh(0.5 * z) + 0.5


def row_sum(v):
    return jnp.sum(v, axis=0, keepdims=True)


def row(ref, index):
    return ref[pl.ds(index, 1), :]


def put_shifted(ref, slot, wide, left_first):
    column = lax.broadcasted_iota(jnp.int32, wide.shape, 0) & (SIDE - 1)
    from_left = jnp.where(column == 0, 0.0, pltpu.roll(wide, 1, 0)).astype(BF)
    from_right = jnp.where(column == SIDE - 1, 0.0, pltpu.roll(wide, POS - 1, 0)).astype(BF)
    first, last = (from_left, from_right) if left_first else (from_right, from_left)
    ref[slot, SIDE : SIDE + POS, 0:C] = first
    ref[slot, SIDE : SIDE + POS, C : 2 * C] = wide.astype(BF)
    ref[slot, SIDE : SIDE + POS, 2 * C : 3 * C] = last


def clear_edges(ref):
    edge = jnp.zeros((SIDE, 3 * C), BF)
    for slot in range(OWN // 2):
        ref[slot, 0:SIDE, :] = edge
        ref[slot, SIDE + POS : PAD, :] = edge


def conv(ref, slot, weights, backward):
    starts = [SIDE * (2 - a) if backward else SIDE * a for a in range(3)]
    window = jnp.concatenate(
        [
            ref[pl.ds(slot, 2), start : start + POS, :].reshape(2 * POS, 3 * C)
            for start in starts
        ],
        axis=1,
    )
    return mm(window, weights[...]).reshape(2, POS, C)


def put_block(out, index, value):
    out[index * C : (index + 1) * C, :] = value.astype(BF)


def weight_taps(out, first, a, transposed, shifted):
    rows = slice(SIDE * (2 - a), SIDE * (2 - a) + POS)
    for b in range(3):
        right = jnp.concatenate(
            [
                ref[:, rows, b * C : (b + 1) * C].reshape(OWN // 2 * POS, C)
                for ref in shifted
            ]
        )
        put_block(out, first + a * 3 + b, mm(transposed[...], right))


def columns_of(place):
    return slice(place * POS, (place + 1) * POS)


def overlapped(ahead, after):
    def both(pair):
        for index in range(2):
            ahead(2 * pair + index, pair % 2, pair // 2 * 2 + index)

    both(0)
    for pair in range(1, OWN // 2):
        both(pair)
        after(2 * pair - 2, (pair - 1) % 2, (pair - 1) // 2 * 2)
    after(OWN - 2, 1, OWN // 2 - 2)


def kernel_body(
    place, steps, own_x, own_g, got, emb, dense, k1, k2, w_in, w_out,
    v0, v1, v2, v3, v4, v5, v6, v7, v8, v9, v10,
    result, result_send, input_own, input_send, grads_keep, grads_send,
    x_ref, g_ref, at_ref, et_ref, a3_even, a3_odd, e3_even, e3_odd, c1_ref, d1_ref, d2_ref, r_ref,
    nt_ref, ot_ref, dq_ref, dn_ref, z_ref, dr_ref, res_ref, send_ref, k1_ref, k2_ref, k1t, k2t,
    emb_ref, dense_ref, steps_grad, grads, small, sums, st, coef, added, vec, sem,
):
    core = lax.rem(place[0], 2)
    base = place[0] * OWN
    mine = pl.ds(core * OWN, OWN)
    a3 = (a3_even, a3_odd)
    e3 = (e3_even, e3_odd)
    copies = [
        pltpu.make_async_copy(own_x.at[mine], x_ref.at[:, core], sem.at[0]),
        pltpu.make_async_copy(got.at[0:OWN], x_ref.at[:, 1 - core], sem.at[1]),
        pltpu.make_async_copy(k1, k1_ref, sem.at[2]),
        pltpu.make_async_copy(dense, dense_ref, sem.at[4]),
        pltpu.make_async_copy(k2, k2_ref, sem.at[5]),
        pltpu.make_async_copy(own_g.at[mine], g_ref.at[:, core], sem.at[6]),
        pltpu.make_async_copy(got.at[OWN:], g_ref.at[:, 1 - core], sem.at[7]),
    ]
    for copy in copies:
        copy.start()
    eights = []
    for m in range(OWN):
        first = pl.multiple_of(steps[base + m] // 8 * 8, 8)
        copy = pltpu.make_async_copy(emb.at[pl.ds(first, 8)], emb_ref.at[m], sem.at[16 + m])
        copy.start()
        eights.append(copy)
    for index, ref in enumerate((v0, v1, v2, v3, v4, v5, v6, v7, v8, v9, v10)):
        vec[index : index + 1, :] = ref[...].reshape(1, C)
    for ref in a3 + e3:
        clear_edges(ref)
    small[...] = jnp.zeros_like(small)
    grads[BLOCKS * C + 16 :, :] = jnp.zeros((ROWS - BLOCKS * C - 16, C), BF)
    steps_grad[...] = jnp.zeros_like(steps_grad)

    def param(index):
        return vec[index : index + 1, :]

    def load_x(m):
        return x_ref[m].reshape(POS, C).astype(F32)

    def load_g(m):
        return g_ref[m].reshape(POS, C)

    def put_sums(m, first, second):
        sums[0, pl.ds(m, 1), :] = row_sum(first)
        sums[1, pl.ds(m, 1), :] = row_sum(second)

    copies[0].wait()
    copies[1].wait()

    for m in range(OWN):
        x = load_x(m)
        put_sums(m, x, x * x)

    mu, rs = statistics(sums[0], sums[1])
    st[MU1] = mu
    st[RS1] = rs
    coef[0] = rs * param(G1)

    for copy in copies[2:4] + eights:
        copy.wait()
    u = jnp.concatenate(
        [emb_ref[m, pl.ds(lax.rem(steps[base + m], 8), 1), :] for m in range(OWN)], axis=0
    )
    w = (u * logistic(u)).astype(BF)
    added[...] = mm(w, dense_ref[...]) + param(B1)

    def transpose_block(to, from_, index):
        at = columns_of(index)
        to[at, :] = from_[at, :].T

    def activate(from_, deriv, transposed, shifted, mu, shift):
        def ahead(m, parity, slot):
            z = (from_(m) - row(mu, m)) * row(coef.at[0], m) + shift
            s = logistic(z)
            a = z * s
            deriv[m] = (s + a * (1.0 - s)).astype(BF)
            transposed[:, columns_of(slot + parity * (OWN // 2))] = a.astype(BF).T
            put_shifted(shifted[parity], slot, a, True)

        return ahead

    def first_conv(m, parity, slot):
        both = conv(a3[parity], slot, k1_ref, False)
        for index in range(2):
            transpose_block(k1t, k1_ref, m + index)
            c1 = both[index] + row(added, m + index)
            c1_ref[m + index] = c1
            put_sums(m + index, c1, c1 * c1)

    overlapped(activate(load_x, d1_ref, at_ref, a3, st.at[MU1], param(S1)), first_conv)
    transpose_block(k1t, k1_ref, 8)

    mu, rs = statistics(sums[0], sums[1])
    st[MU2] = mu
    st[RS2] = rs
    coef[0] = rs * param(G2)
    copies[4].wait()

    def second_conv(m, parity, slot):
        both = conv(e3[parity], slot, k2_ref, False)
        for index in range(2):
            transpose_block(k2t, k2_ref, m + index)
            r = load_x(m + index) + both[index] + param(B2)
            r_ref[m + index] = r
            put_sums(m + index, r, r * r)

    overlapped(
        activate(lambda m: c1_ref[m], d2_ref, et_ref, e3, st.at[MU2], param(S2)), second_conv
    )
    transpose_block(k2t, k2_ref, 8)

    mu, rs = statistics(sums[0], sums[1])
    coef[0] = mu
    coef[1] = rs
    coef[2] = rs * param(G3)
    copies[5].wait()
    copies[6].wait()

    def two(rows):
        return [rows[0:POS], rows[POS : 2 * POS]]

    def attention(pair):
        maps = [2 * pair, 2 * pair + 1]
        scale = C ** (-0.5)
        r = [r_ref[m] for m in maps]
        t = [v - row(coef.at[0], m) for v, m in zip(r, maps)]
        n = [(v * row(coef.at[2], m) + param(S3)).astype(BF) for v, m in zip(t, maps)]
        for v, m in zip(n, maps):
            nt_ref[:, columns_of(m)] = v.T
        joined = two(mm(jnp.concatenate(n), w_in[...]))
        q = [
            ((v[:, 0:C] + param(BQ)).astype(BF).astype(F32) * scale).astype(BF) for v in joined
        ]
        k = [v[:, C : 2 * C].astype(BF) for v in joined]
        v = [b[:, 2 * C :] + param(BV) for b in joined]
        v = [b.astype(BF) for b in v]
        g = [load_g(m) for m in maps]
        do = two(mm_nt(jnp.concatenate(g), w_out[...]).astype(BF))
        scores = [mm_nt(a, b) for a, b in zip(k, q)]
        dp = [mm_nt(a, b) for a, b in zip(v, do)]
        e = [jnp.exp(a - jnp.max(a, axis=0, keepdims=True)) for a in scores]
        p = [a * (1.0 / jnp.sum(a, axis=0, keepdims=True)) for a in e]
        low = [a.astype(BF) for a in p]
        ds = [(a * (b - row_sum(a * b))).astype(BF) for a, b in zip(p, dp)]
        o = [mm_tn(a, b).astype(BF) for a, b in zip(low, v)]
        dv = [mm(a, b).astype(BF) for a, b in zip(low, do)]
        dk = [mm(a, b).astype(BF) for a, b in zip(ds, q)]
        dq = [(mm_tn(a, b) * scale).astype(BF) for a, b in zip(ds, k)]
        for m, a in zip(maps, o):
            ot_ref[:, columns_of(m)] = a.T
        for m, a, b in zip(maps, r, two(mm(jnp.concatenate(o), w_out[...]))):
            res = a + b + param(BO)
            res_ref[m] = res.astype(BF).reshape(2, HALF, C)
        together = [jnp.concatenate(parts, axis=1) for parts in zip(dq, dk, dv)]
        dn = two(mm_nt(jnp.concatenate(together), w_in[...]))
        for m, a, b, c in zip(maps, together, dn, t):
            dq_ref[m] = a
            dn_ref[m] = b
            put_sums(m, b, b * (c * row(coef.at[1], m)))
        for index, parts in enumerate((dq, dv, g)):
            total = row_sum(parts[0].astype(F32)) + row_sum(parts[1].astype(F32))
            small[index : index + 1, :] += total

    for pair in range(OWN // 2):
        attention(pair)

    give = [
        pltpu.make_async_copy(res_ref.at[:, core], result.at[mine], sem.at[8]),
        pltpu.make_async_copy(res_ref.at[:, 1 - core], result_send, sem.at[9]),
    ]
    for copy in give:
        copy.start()

    def finish_norm(rs, gain, at):
        small[at : at + 1, :] = row_sum(sums[1])
        small[at + 1 : at + 2, :] = row_sum(sums[0])
        coef[2] = rs * gain
        coef[3] = rs * rs * group_total(sums[1] * gain) * (1.0 / COUNT)
        coef[4] = rs * group_total(sums[0] * gain) * (1.0 / COUNT)

    def norm_grad(g, t, m):
        return g * row(coef.at[2], m) - t * row(coef.at[3], m) - row(coef.at[4], m)

    finish_norm(coef[1], param(G3), 3)

    def mixer_back(m, parity, slot):
        dr = load_g(m).astype(F32) + norm_grad(dn_ref[m], r_ref[m] - row(coef.at[0], m), m)
        dr_ref[m] = dr
        low = dr.astype(BF).astype(F32)
        small[5:6, :] += row_sum(low)
        put_shifted(a3[parity], slot, low, False)

    def second_back(m, parity, slot):
        both = conv(a3[parity], slot, k2t, True)
        for index in range(2):
            at = m + index
            g = both[index] * d2_ref[at].astype(F32)
            z_ref[at] = g
            put_sums(at, g, g * ((c1_ref[at] - row(st.at[MU2], at)) * row(st.at[RS2], at)))

    overlapped(mixer_back, second_back)

    for a in range(3):
        weight_taps(grads, 0, a, et_ref, a3)
    flat = dq_ref[...].reshape(OWN * POS, 3 * C)
    for part in range(3):
        put_block(grads, 9 + part, mm(nt_ref[...], flat[:, part * C : (part + 1) * C]))
    put_block(grads, 12, mm(ot_ref[...], g_ref[...].reshape(OWN * POS, C)))

    def leave_low(to):
        return pltpu.make_async_copy(grads.at[0:PART], to, sem.at[12])

    def leave_high(at, rows, index):
        def to(ref):
            source = grads.at[PART + at : PART + at + rows]
            return pltpu.make_async_copy(source, ref.at[at : at + rows], sem.at[index])

        return to

    @pl.when(core == 0)
    def _():
        leave_low(grads_keep).start()

    @pl.when(core == 1)
    def _():
        leave_low(grads_send).start()

    finish_norm(st[RS2], param(G2), 6)

    def hidden_back(m, parity, slot):
        t = c1_ref[m] - row(st.at[MU2], m)
        low = norm_grad(z_ref[m], t, m).astype(BF).astype(F32)
        total = row_sum(low)
        small[8:9, :] += total
        where = pl.ds(steps[base + m], 1)
        steps_grad[where, :] = steps_grad[where, :] + total
        put_shifted(e3[parity], slot, low, False)

    def centered(m):
        return load_x(m) - row(st.at[MU1], m)

    def first_back(m, parity, slot):
        both = conv(e3[parity], slot, k1t, True)
        for index in range(2):
            at = m + index
            g = both[index] * d1_ref[at].astype(F32)
            dn_ref[at] = g
            put_sums(at, g, g * (centered(at) * row(st.at[RS1], at)))

    overlapped(hidden_back, first_back)
    put_block(grads, 22, steps_grad[...])
    finish_norm(st[RS1], param(G1), 9)
    grads[BLOCKS * C : BLOCKS * C + 16, :] = small[...].astype(BF)
    away = pl.ds((1 - core) * HALF, HALF)

    def input_back(m):
        r_ref[m] = dr_ref[m] + norm_grad(dn_ref[m], centered(m), m)
        send_ref[m] = r_ref[m, away, :].astype(BF)

    for a in range(2):
        for index in range(3):
            input_back(3 * a + index)
        weight_taps(grads, 13, a, at_ref, e3)

    pieces = [leave_high(0, 7 * C, 14), leave_high(7 * C, PART - 7 * C, 15)]

    @pl.when(core == 0)
    def _():
        pieces[0](grads_send).start()

    @pl.when(core == 1)
    def _():
        pieces[0](grads_keep).start()

    input_back(6)
    input_back(7)
    give += [
        pltpu.make_async_copy(r_ref.at[:, pl.ds(core * HALF, HALF)], input_own.at[mine], sem.at[10]),
        pltpu.make_async_copy(send_ref, input_send, sem.at[11]),
    ]
    for copy in give[2:]:
        copy.start()
    weight_taps(grads, 13, 2, at_ref, e3)

    @pl.when(core == 0)
    def _():
        last = pieces[1](grads_send)
        last.start()
        leave_low(grads_keep).wait()
        pieces[0](grads_send).wait()
        last.wait()

    @pl.when(core == 1)
    def _():
        last = pieces[1](grads_keep)
        last.start()
        leave_low(grads_send).wait()
        pieces[0](grads_keep).wait()
        last.wait()

    for copy in give:
        copy.wait()


def shape(*dims, kind=F32):
    return jax.ShapeDtypeStruct(dims, kind)


SMEM = pl.BlockSpec(memory_space=pltpu.SMEM)
VMEM = pl.BlockSpec(memory_space=pltpu.VMEM)
ANY = pl.BlockSpec(memory_space=pl.ANY)
FULL = 60 * 1024 * 1024
ALL = 62 * 1024 * 1024
MOST = 40 * 1024 * 1024
LEAST = 16 * 1024 * 1024
HALF = POS // 2
MAP = (OWN, POS, C)
BANDS = (OWN, 2, HALF, C)
TRIPLE = (OWN // 2, PAD, 3 * C)
WIDE = (C, OWN * POS)
BLOCKS = 23
VECTORS = 11
PEERS = 64
EIGHT = 8
EIGHTH = 384
EVENLY = (1, 2, 4, 7, 3, 5, 6)
PART = EIGHT * EIGHTH
ROWS = 2 * PART


def run(place, steps, own_x, own_g, got, emb, dense, k1, k2, w_in, w_out, vectors):
    return pl.pallas_call(
        kernel_body,
        in_specs=[SMEM, SMEM] + [ANY] * 7 + [VMEM] * 13,
        out_specs=[ANY] * 6,
        out_shape=[
            shape(2 * OWN, HALF, C, kind=BF),
            shape(OWN, HALF, C, kind=BF),
            shape(2 * OWN, HALF, C),
            shape(OWN, HALF, C, kind=BF),
            shape(PART, C, kind=BF),
            shape(PART, C, kind=BF),
        ],
        scratch_shapes=[
            pltpu.VMEM(BANDS, BF),
            pltpu.VMEM(BANDS, BF),
            pltpu.VMEM(WIDE, BF),
            pltpu.VMEM(WIDE, BF),
            pltpu.VMEM(TRIPLE, BF),
            pltpu.VMEM(TRIPLE, BF),
            pltpu.VMEM(TRIPLE, BF),
            pltpu.VMEM(TRIPLE, BF),
            pltpu.VMEM(MAP, F32),
            pltpu.VMEM(MAP, BF),
            pltpu.VMEM(MAP, BF),
            pltpu.VMEM(MAP, F32),
            pltpu.VMEM(WIDE, BF),
            pltpu.VMEM(WIDE, BF),
            pltpu.VMEM((OWN, POS, 3 * C), BF),
            pltpu.VMEM(MAP, F32),
            pltpu.VMEM(MAP, F32),
            pltpu.VMEM(MAP, F32),
            pltpu.VMEM(BANDS, BF),
            pltpu.VMEM((OWN, HALF, C), BF),
            pltpu.VMEM((9 * C, C), BF),
            pltpu.VMEM((9 * C, C), BF),
            pltpu.VMEM((9 * C, C), BF),
            pltpu.VMEM((9 * C, C), BF),
            pltpu.VMEM((OWN, 8, 4 * C), F32),
            pltpu.VMEM((4 * C, C), BF),
            pltpu.VMEM((C, C), F32),
            pltpu.VMEM((ROWS, C), BF),
            pltpu.VMEM((16, C), F32),
            pltpu.VMEM((2, OWN, C), F32),
            pltpu.VMEM((4, OWN, C), F32),
            pltpu.VMEM((5, OWN, C), F32),
            pltpu.VMEM((OWN, C), F32),
            pltpu.VMEM((16, C), F32),
            pltpu.SemaphoreType.DMA((16 + OWN,)),
        ],
        compiler_params=pltpu.CompilerParams(vmem_limit_bytes=FULL),
        cost_estimate=pl.CostEstimate(
            flops=20 * 10**9, bytes_accessed=20 * 10**6, transcendentals=3 * 10**6
        ),
    )(place, steps, own_x, own_g, got, emb, dense, k1, k2, w_in, w_out, *vectors)


def swap(block):
    count = lax.axis_size("batch")
    return lax.ppermute(block, "batch", [(i, i ^ 1) for i in range(count)])


def join_body(place, mine_r, mine_i, got_r, got_i, out_r, out_i, wide_i, sem):
    there = pl.ds((1 - lax.rem(place[0], 2)) * OWN, OWN)
    first = pltpu.make_async_copy(got_r, out_r.at[there], sem.at[0])
    first.start()
    wide_i[...] = got_i[...].astype(F32)
    second = pltpu.make_async_copy(wide_i, out_i.at[there], sem.at[1])
    second.start()
    first.wait()
    second.wait()


def join(place, mine_r, mine_i, got_r, got_i):
    return pl.pallas_call(
        join_body,
        in_specs=[SMEM, ANY, ANY, ANY, VMEM],
        out_specs=[ANY, ANY],
        out_shape=[shape(*mine_r.shape, kind=BF), shape(*mine_i.shape)],
        input_output_aliases={1: 0, 2: 1},
        scratch_shapes=[pltpu.VMEM((OWN, HALF, C), F32), pltpu.SemaphoreType.DMA((2,))],
        compiler_params=pltpu.CompilerParams(vmem_limit_bytes=LEAST),
        cost_estimate=pl.CostEstimate(flops=0, bytes_accessed=4 * 10**6, transcendentals=0),
    )(place, mine_r, mine_i, got_r, got_i)


def load_body(x, out, sem):
    copy = pltpu.make_async_copy(x, out, sem)
    copy.start()
    copy.wait()


def nearby(x):
    return pl.pallas_call(
        load_body,
        in_specs=[ANY],
        out_specs=VMEM,
        out_shape=shape(*x.shape, kind=x.dtype),
        scratch_shapes=[pltpu.SemaphoreType.DMA],
        compiler_params=pltpu.CompilerParams(vmem_limit_bytes=LEAST),
        cost_estimate=pl.CostEstimate(flops=0, bytes_accessed=2 * 10**6, transcendentals=0),
    )(x)


def wide(ref):
    return ref[...].astype(F32)


def eighth_of(index):
    return pl.ds(pl.multiple_of(index * EIGHTH, EIGHTH), EIGHTH)


def add_body(piece, mine, other, *outs):
    for mask in range(EIGHT):
        at = eighth_of(piece[0] ^ mask)
        total = mine[at, :].astype(F32) + other[at, :].astype(F32)
        outs[mask][...] = total.astype(BF)


def eight_body(*refs):
    total = wide(refs[0])
    for ref in refs[1:EIGHT]:
        total = total + wide(ref)
    low = total.astype(BF)
    for index, out in enumerate(refs[EIGHT:]):
        out[...] = low[index * (EIGHTH // 2) : (index + 1) * (EIGHTH // 2), :]


def two_body(mine, got, out):
    out[...] = (wide(mine) + wide(got)).astype(BF)


def last_body(mine_a, got_a, mine_b, got_b, out):
    out[0 : EIGHTH // 2, :] = (wide(mine_a) + wide(got_a)).astype(BF)
    out[EIGHTH // 2 :, :] = (wide(mine_b) + wide(got_b)).astype(BF)


def place_body(piece, *refs):
    for index, mask in enumerate((0,) + EVENLY):
        refs[EIGHT][eighth_of(piece[0] ^ mask), :] = refs[index][...]


def small_call(kernel, rows, count, *operands):
    scalars = [SMEM] if operands[0].ndim == 1 else []
    return pl.pallas_call(
        kernel,
        in_specs=scalars + [VMEM] * (len(operands) - len(scalars)),
        out_specs=[VMEM] * count,
        out_shape=[shape(rows, C, kind=BF)] * count,
        compiler_params=pltpu.CompilerParams(vmem_limit_bytes=LEAST),
        cost_estimate=pl.CostEstimate(flops=10**6, bytes_accessed=10**6, transcendentals=0),
    )(*operands)


def shifts(core):
    return [core, core, 1 - core]


def lines(index):
    return [
        (index // 2 // 4**axis + 3 * shift) % 4 for axis, shift in enumerate(shifts(index % 2))
    ]


def device_at(places, core):
    chip = sum(
        (place + shift) % 4 * 4**axis
        for axis, (place, shift) in enumerate(zip(places, shifts(core)))
    )
    return 2 * chip + core


def exchange(block, moved):
    pairs = [
        (index, device_at(moved(lines(index)), index % 2)) for index in range(2 * PEERS)
    ]
    return lax.ppermute(block, "batch", pairs)


def near(mask):
    return lambda places: [p ^ (mask >> axis & 1) for axis, p in enumerate(places)]


def far(axis):
    return lambda places: [3 - p if at == axis else p for at, p in enumerate(places)]


def all_sum(keep, other, device, meanwhile, afterwards):
    bits = [(place + 1) // 2 % 2 for place in lines(device)]
    piece = (bits[0] + 2 * bits[1] + 4 * bits[2]).reshape(1).astype(jnp.int32)
    sends = small_call(add_body, EIGHTH, EIGHT, piece, nearby(keep), other)
    arrived = meanwhile(sends[0])
    early, late = EVENLY[:3], EVENLY[3:]
    got = [exchange(sends[mask], near(mask)) for mask in early]
    held, arrived = lax.optimization_barrier(([sends[mask] for mask in late], arrived))
    got += [exchange(block, near(mask)) for block, mask in zip(held, late)]
    first, beside = lax.optimization_barrier((sends[0], afterwards(arrived)))
    a, b = small_call(eight_body, EIGHTH // 2, 2, first, *got)
    for step in range(2):
        a, b = (
            small_call(two_body, EIGHTH // 2, 1, part, exchange(part, far((step + first) % 3)))[0]
            for first, part in enumerate((a, b))
        )
    whole = small_call(
        last_body, EIGHTH, 1, a, exchange(a, far(2)), b, exchange(b, far(0))
    )[0]
    got = [exchange(whole, near(mask)) for mask in EVENLY]
    mine = small_call(place_body, PART, 1, piece, whole, *got)[0]
    return mine, swap(mine), beside


def write_half(high, part, emb, dense, outs, stage, wide_stage, table, emb_ref, dense_ref, sem):
    second_grad, in_grad, out_grad, first_grad, dense_grad, emb_grad = outs
    if high:
        places = [out_grad] + [first_grad.at[index] for index in range(9)]
        fetch = [
            pltpu.make_async_copy(emb, emb_ref, sem.at[18]),
            pltpu.make_async_copy(dense, dense_ref, sem.at[19]),
        ]
        for copy in fetch:
            copy.start()
    else:
        places = [second_grad.at[index] for index in range(9)]
        places += [in_grad.at[:, index * C : (index + 1) * C] for index in range(3)]
    copies = []

    def leave(source, to):
        copy = pltpu.make_async_copy(source, to, sem.at[len(copies)])
        copy.start()
        copies.append(copy)

    for index, to in enumerate(places):
        stage[index] = part[index * C : (index + 1) * C, :].astype(F32)
        leave(stage.at[index], to)
    if high:
        table[...] = part[10 * C : 11 * C, :]
        for copy in fetch:
            copy.wait()
        for index in range(4):
            columns = slice(index * C, (index + 1) * C)
            u = emb_ref[:, columns]
            s = logistic(u)
            active = u * s
            wide_stage[0, index] = mm(active.astype(BF).T, table[...])
            leave(wide_stage.at[0, index], dense_grad.at[columns, :])
            slope = s + active * (1.0 - s)
            wide_stage[1, index] = mm_nt(table[...], dense_ref[columns, :]) * slope
            leave(wide_stage.at[1, index], emb_grad.at[:, columns])
    for copy in copies:
        copy.wait()


def finish_own_body(place, mine, emb, dense, *refs):
    outs, scratch = refs[:6], refs[6:]
    for core in range(2):

        @pl.when(lax.rem(place[0], 2) == core)
        def _():
            write_half(core == 1, mine, emb, dense, outs, *scratch)


def finish_other_body(place, mine, other, emb, dense, *refs):
    outs, vectors, scratch = refs[6:12], refs[12 : 12 + VECTORS], refs[12 + VECTORS :]
    core = lax.rem(place[0], 2)
    at = slice(11 * C, 11 * C + 16)
    rows = jnp.where(core == 1, mine[at, :].astype(F32), other[at, :].astype(F32))
    for index, out in enumerate(vectors):
        out[...] = rows[index : index + 1, :].reshape(C)
    for this in range(2):

        @pl.when(core == this)
        def _():
            write_half(this == 0, other, emb, dense, outs, *scratch)


def finish(place, mine, other, emb, dense):
    dims = [(9, C, C), (C, 3 * C), (C, C), (9, C, C), (4 * C, C), (C, 4 * C)]
    settings = dict(
        scratch_shapes=[
            pltpu.VMEM((12, C, C), F32),
            pltpu.VMEM((2, 4, C, C), F32),
            pltpu.VMEM((C, C), BF),
            pltpu.VMEM((C, 4 * C), F32),
            pltpu.VMEM((4 * C, C), BF),
            pltpu.SemaphoreType.DMA((20,)),
        ],
        compiler_params=pltpu.CompilerParams(vmem_limit_bytes=LEAST),
        cost_estimate=pl.CostEstimate(
            flops=10**8, bytes_accessed=6 * 10**6, transcendentals=10**5
        ),
    )
    outs = pl.pallas_call(
        finish_own_body,
        in_specs=[SMEM, VMEM, ANY, ANY],
        out_specs=[ANY] * 6,
        out_shape=[shape(*d) for d in dims],
        **settings,
    )(place, mine, emb, dense)
    return pl.pallas_call(
        finish_other_body,
        in_specs=[SMEM, VMEM, VMEM, ANY, ANY] + [ANY] * 6,
        out_specs=[ANY] * 6 + [VMEM] * VECTORS,
        out_shape=[shape(*d) for d in dims] + [shape(C)] * VECTORS,
        input_output_aliases={5 + index: index for index in range(6)},
        **settings,
    )(place, mine, other, emb, dense, *outs)


def body(
    features, timesteps, embedding, first_gain, first_shift, first_kernel, first_bias, time_dense,
    second_gain, second_shift, second_kernel, second_bias, mixer_gain, mixer_shift, project_in,
    query_bias, value_bias, project_out, output_bias, cotangent,
):
    device = lax.axis_index("batch")
    own_x = features.reshape(2 * OWN, HALF, C)
    own_g = cotangent.reshape(2 * OWN, HALF, C)
    there = (1 - device % 2) * OWN
    place = device.reshape(1).astype(jnp.int32)
    got = swap(
        jnp.concatenate(
            [
                lax.dynamic_slice_in_dim(own_x, there, OWN),
                lax.dynamic_slice_in_dim(own_g, there, OWN),
            ]
        )
    )
    vectors = (
        first_gain, first_shift, first_bias, second_gain, second_shift, second_bias,
        mixer_gain, mixer_shift, query_bias, value_bias, output_bias,
    )
    result, result_send, input_grad, input_send, keep, send = run(
        place, timesteps, own_x, own_g, got, embedding, time_dense,
        first_kernel.reshape(9 * C, C), second_kernel.reshape(9 * C, C), project_in, project_out,
        vectors,
    )
    def swap_maps(block):
        first, second, _ = lax.optimization_barrier((result_send, input_send, block))
        return swap(first), swap(second)

    def join_maps(arrived):
        return join(place, result, input_grad, *arrived)

    mine, other, (result, input_grad) = all_sum(keep, swap(send), device, swap_maps, join_maps)
    (
        second_kernel_grad, in_grad, out_grad, first_kernel_grad, time_dense_grad, embedding_grad,
        *rows,
    ) = finish(place, mine, other, embedding, time_dense)
    banded = features.shape
    return (
        result.reshape(banded),
        input_grad.reshape(banded),
        embedding_grad,
        rows[9],
        rows[10],
        first_kernel_grad.reshape(3, 3, C, C),
        rows[8],
        time_dense_grad,
        rows[6],
        rows[7],
        second_kernel_grad.reshape(3, 3, C, C),
        rows[5],
        rows[3],
        rows[4],
        in_grad,
        rows[0],
        rows[1],
        out_grad,
        rows[2],
    )


def solution(mesh):
    split = P("batch", None, None, None, None)
    return jax.shard_map(
        body,
        mesh=mesh,
        in_specs=(split,) + (P(),) * 18 + (split,),
        out_specs=(split, split) + (P(),) * 17,
        check_vma=False,
    )
```

```python
import jax
import jax.numpy as jnp
from jax import lax
from jax.experimental import pallas as pl
from jax.experimental.pallas import tpu as pltpu
from jax.sharding import PartitionSpec as P

BF = jnp.bfloat16
F32 = jnp.float32
C = 256
SIDE = 16
POS = 256
GROUPS = 32
LANES = 128
EPSILON = 1e-05
OWN = 8
PAD = POS + 2 * SIDE
COUNT = float(POS * C // GROUPS)

G1, S1, B1, G2, S2, B2, G3, S3, BQ, BV, BO = range(11)
MU1, RS1, MU2, RS2 = range(4)


def mm(a, b):
    return jnp.dot(a, b, preferred_element_type=F32)


def mm_nt(a, b):
    return lax.dot_general(a, b, (((1,), (1,)), ((), ())), preferred_element_type=F32)


def mm_tn(a, b):
    return lax.dot_general(a, b, (((0,), (0,)), ((), ())), preferred_element_type=F32)


def group_total(s):
    lane = lax.broadcasted_iota(jnp.int32, s.shape, 1)
    for bit in (1, 2, 4):
        s = s + jnp.where((lane & bit) == 0, pltpu.roll(s, C - bit, 1), pltpu.roll(s, bit, 1))
    return s


def statistics(total, squares):
    mu = group_total(total) * (1.0 / COUNT)
    var = group_total(squares) * (1.0 / COUNT) - mu * mu
    return mu, lax.rsqrt(var + EPSILON)


def logistic(z):
    return 0.5 * jnp.tanh(0.5 * z) + 0.5


def row_sum(v):
    return jnp.sum(v, axis=0, keepdims=True)


def row(ref, index):
    return ref[pl.ds(index, 1), :]


def put_shifted(ref, slot, wide, left_first):
    column = lax.broadcasted_iota(jnp.int32, wide.shape, 0) & (SIDE - 1)
    from_left = jnp.where(column == 0, 0.0, pltpu.roll(wide, 1, 0)).astype(BF)
    from_right = jnp.where(column == SIDE - 1, 0.0, pltpu.roll(wide, POS - 1, 0)).astype(BF)
    first, last = (from_left, from_right) if left_first else (from_right, from_left)
    ref[slot, SIDE : SIDE + POS, 0:C] = first
    ref[slot, SIDE : SIDE + POS, C : 2 * C] = wide.astype(BF)
    ref[slot, SIDE : SIDE + POS, 2 * C : 3 * C] = last


def clear_edges(ref):
    edge = jnp.zeros((SIDE, 3 * C), BF)
    for slot in range(OWN // 2):
        ref[slot, 0:SIDE, :] = edge
        ref[slot, SIDE + POS : PAD, :] = edge


def conv(ref, slot, weights, backward):
    starts = [SIDE * (2 - a) if backward else SIDE * a for a in range(3)]
    window = jnp.concatenate(
        [
            ref[pl.ds(slot, 2), start : start + POS, :].reshape(2 * POS, 3 * C)
            for start in starts
        ],
        axis=1,
    )
    return mm(window, weights[...]).reshape(2, POS, C)


def put_block(out, index, value):
    out[index * C : (index + 1) * C, :] = value.astype(BF)


def weight_taps(out, first, a, transposed, shifted):
    rows = slice(SIDE * (2 - a), SIDE * (2 - a) + POS)
    for b in range(3):
        right = jnp.concatenate(
            [
                ref[:, rows, b * C : (b + 1) * C].reshape(OWN // 2 * POS, C)
                for ref in shifted
            ]
        )
        put_block(out, first + a * 3 + b, mm(transposed[...], right))


def columns_of(place):
    return slice(place * POS, (place + 1) * POS)


def overlapped(ahead, after):
    def both(pair):
        for index in range(2):
            ahead(2 * pair + index, pair % 2, pair // 2 * 2 + index)

    both(0)
    for pair in range(1, OWN // 2):
        both(pair)
        after(2 * pair - 2, (pair - 1) % 2, (pair - 1) // 2 * 2)
    after(OWN - 2, 1, OWN // 2 - 2)


def kernel_body(
    place, steps, own_x, own_g, got, emb, dense, k1, k2, w_in, w_out,
    v0, v1, v2, v3, v4, v5, v6, v7, v8, v9, v10,
    result, result_send, input_own, input_send, grads_keep, grads_send,
    x_ref, g_ref, at_ref, et_ref, a3_even, a3_odd, e3_even, e3_odd, c1_ref, d1_ref, d2_ref, r_ref,
    nt_ref, ot_ref, dq_ref, dn_ref, z_ref, dr_ref, res_ref, send_ref, k1_ref, k2_ref, k1t, k2t,
    emb_ref, dense_ref, steps_grad, grads, small, sums, st, coef, added, vec, sem,
):
    core = lax.rem(place[0], 2)
    base = place[0] * OWN
    mine = pl.ds(core * OWN, OWN)
    a3 = (a3_even, a3_odd)
    e3 = (e3_even, e3_odd)
    copies = [
        pltpu.make_async_copy(own_x.at[mine], x_ref.at[:, core], sem.at[0]),
        pltpu.make_async_copy(got.at[0:OWN], x_ref.at[:, 1 - core], sem.at[1]),
        pltpu.make_async_copy(k1, k1_ref, sem.at[2]),
        pltpu.make_async_copy(dense, dense_ref, sem.at[4]),
        pltpu.make_async_copy(k2, k2_ref, sem.at[5]),
        pltpu.make_async_copy(own_g.at[mine], g_ref.at[:, core], sem.at[6]),
        pltpu.make_async_copy(got.at[OWN:], g_ref.at[:, 1 - core], sem.at[7]),
    ]
    for copy in copies:
        copy.start()
    eights = []
    for m in range(OWN):
        first = pl.multiple_of(steps[base + m] // 8 * 8, 8)
        copy = pltpu.make_async_copy(emb.at[pl.ds(first, 8)], emb_ref.at[m], sem.at[16 + m])
        copy.start()
        eights.append(copy)
    for index, ref in enumerate((v0, v1, v2, v3, v4, v5, v6, v7, v8, v9, v10)):
        vec[index : index + 1, :] = ref[...].reshape(1, C)
    for ref in a3 + e3:
        clear_edges(ref)
    small[...] = jnp.zeros_like(small)
    grads[BLOCKS * C + 16 :, :] = jnp.zeros((ROWS - BLOCKS * C - 16, C), BF)
    steps_grad[...] = jnp.zeros_like(steps_grad)

    def param(index):
        return vec[index : index + 1, :]

    def load_x(m):
        return x_ref[m].reshape(POS, C).astype(F32)

    def load_g(m):
        return g_ref[m].reshape(POS, C)

    def put_sums(m, first, second):
        sums[0, pl.ds(m, 1), :] = row_sum(first)
        sums[1, pl.ds(m, 1), :] = row_sum(second)

    copies[0].wait()
    copies[1].wait()

    for m in range(OWN):
        x = load_x(m)
        put_sums(m, x, x * x)

    mu, rs = statistics(sums[0], sums[1])
    st[MU1] = mu
    st[RS1] = rs
    coef[0] = rs * param(G1)

    for copy in copies[2:4] + eights:
        copy.wait()
    u = jnp.concatenate(
        [emb_ref[m, pl.ds(lax.rem(steps[base + m], 8), 1), :] for m in range(OWN)], axis=0
    )
    w = (u * logistic(u)).astype(BF)
    added[...] = mm(w, dense_ref[...]) + param(B1)

    def transpose_block(to, from_, index):
        at = columns_of(index)
        to[at, :] = from_[at, :].T

    def activate(from_, deriv, transposed, shifted, mu, shift):
        def ahead(m, parity, slot):
            z = (from_(m) - row(mu, m)) * row(coef.at[0], m) + shift
            s = logistic(z)
            a = z * s
            deriv[m] = (s + a * (1.0 - s)).astype(BF)
            transposed[:, columns_of(slot + parity * (OWN // 2))] = a.astype(BF).T
            put_shifted(shifted[parity], slot, a, True)

        return ahead

    def first_conv(m, parity, slot):
        both = conv(a3[parity], slot, k1_ref, False)
        for index in range(2):
            transpose_block(k1t, k1_ref, m + index)
            c1 = both[index] + row(added, m + index)
            c1_ref[m + index] = c1
            put_sums(m + index, c1, c1 * c1)

    overlapped(activate(load_x, d1_ref, at_ref, a3, st.at[MU1], param(S1)), first_conv)
    transpose_block(k1t, k1_ref, 8)

    mu, rs = statistics(sums[0], sums[1])
    st[MU2] = mu
    st[RS2] = rs
    coef[0] = rs * param(G2)
    copies[4].wait()

    def second_conv(m, parity, slot):
        both = conv(e3[parity], slot, k2_ref, False)
        for index in range(2):
            transpose_block(k2t, k2_ref, m + index)
            r = load_x(m + index) + both[index] + param(B2)
            r_ref[m + index] = r
            put_sums(m + index, r, r * r)

    overlapped(
        activate(lambda m: c1_ref[m], d2_ref, et_ref, e3, st.at[MU2], param(S2)), second_conv
    )
    transpose_block(k2t, k2_ref, 8)

    mu, rs = statistics(sums[0], sums[1])
    coef[0] = mu
    coef[1] = rs
    coef[2] = rs * param(G3)
    copies[5].wait()
    copies[6].wait()

    def two(rows):
        return [rows[0:POS], rows[POS : 2 * POS]]

    def attention(pair):
        maps = [2 * pair, 2 * pair + 1]
        scale = C ** (-0.5)
        r = [r_ref[m] for m in maps]
        t = [v - row(coef.at[0], m) for v, m in zip(r, maps)]
        n = [(v * row(coef.at[2], m) + param(S3)).astype(BF) for v, m in zip(t, maps)]
        for v, m in zip(n, maps):
            nt_ref[:, columns_of(m)] = v.T
        joined = two(mm(jnp.concatenate(n), w_in[...]))
        q = [
            ((v[:, 0:C] + param(BQ)).astype(BF).astype(F32) * scale).astype(BF) for v in joined
        ]
        k = [v[:, C : 2 * C].astype(BF) for v in joined]
        v = [b[:, 2 * C :] + param(BV) for b in joined]
        v = [b.astype(BF) for b in v]
        g = [load_g(m) for m in maps]
        do = two(mm_nt(jnp.concatenate(g), w_out[...]).astype(BF))
        scores = [mm_nt(a, b) for a, b in zip(k, q)]
        dp = [mm_nt(a, b) for a, b in zip(v, do)]
        e = [jnp.exp(a - jnp.max(a, axis=0, keepdims=True)) for a in scores]
        p = [a * (1.0 / jnp.sum(a, axis=0, keepdims=True)) for a in e]
        low = [a.astype(BF) for a in p]
        ds = [(a * (b - row_sum(a * b))).astype(BF) for a, b in zip(p, dp)]
        o = [mm_tn(a, b).astype(BF) for a, b in zip(low, v)]
        dv = [mm(a, b).astype(BF) for a, b in zip(low, do)]
        dk = [mm(a, b).astype(BF) for a, b in zip(ds, q)]
        dq = [(mm_tn(a, b) * scale).astype(BF) for a, b in zip(ds, k)]
        for m, a in zip(maps, o):
            ot_ref[:, columns_of(m)] = a.T
        for m, a, b in zip(maps, r, two(mm(jnp.concatenate(o), w_out[...]))):
            res = a + b + param(BO)
            res_ref[m] = res.astype(BF).reshape(2, HALF, C)
        together = [jnp.concatenate(parts, axis=1) for parts in zip(dq, dk, dv)]
        dn = two(mm_nt(jnp.concatenate(together), w_in[...]))
        for m, a, b, c in zip(maps, together, dn, t):
            dq_ref[m] = a
            dn_ref[m] = b
            put_sums(m, b, b * (c * row(coef.at[1], m)))
        for index, parts in enumerate((dq, dv, g)):
            total = row_sum(parts[0].astype(F32)) + row_sum(parts[1].astype(F32))
            small[index : index + 1, :] += total

    for pair in range(OWN // 2):
        attention(pair)

    give = [
        pltpu.make_async_copy(res_ref.at[:, core], result.at[mine], sem.at[8]),
        pltpu.make_async_copy(res_ref.at[:, 1 - core], result_send, sem.at[9]),
    ]
    for copy in give:
        copy.start()

    def finish_norm(rs, gain, at):
        small[at : at + 1, :] = row_sum(sums[1])
        small[at + 1 : at + 2, :] = row_sum(sums[0])
        coef[2] = rs * gain
        coef[3] = rs * rs * group_total(sums[1] * gain) * (1.0 / COUNT)
        coef[4] = rs * group_total(sums[0] * gain) * (1.0 / COUNT)

    def norm_grad(g, t, m):
        return g * row(coef.at[2], m) - t * row(coef.at[3], m) - row(coef.at[4], m)

    finish_norm(coef[1], param(G3), 3)

    def mixer_back(m, parity, slot):
        dr = load_g(m).astype(F32) + norm_grad(dn_ref[m], r_ref[m] - row(coef.at[0], m), m)
        dr_ref[m] = dr
        low = dr.astype(BF).astype(F32)
        small[5:6, :] += row_sum(low)
        put_shifted(a3[parity], slot, low, False)

    def second_back(m, parity, slot):
        both = conv(a3[parity], slot, k2t, True)
        for index in range(2):
            at = m + index
            g = both[index] * d2_ref[at].astype(F32)
            z_ref[at] = g
            put_sums(at, g, g * ((c1_ref[at] - row(st.at[MU2], at)) * row(st.at[RS2], at)))

    overlapped(mixer_back, second_back)

    for a in range(3):
        weight_taps(grads, 0, a, et_ref, a3)
    flat = dq_ref[...].reshape(OWN * POS, 3 * C)
    for part in range(3):
        put_block(grads, 9 + part, mm(nt_ref[...], flat[:, part * C : (part + 1) * C]))
    put_block(grads, 12, mm(ot_ref[...], g_ref[...].reshape(OWN * POS, C)))

    def leave_low(to):
        return pltpu.make_async_copy(grads.at[0:PART], to, sem.at[12])

    def leave_high(at, rows, index):
        def to(ref):
            source = grads.at[PART + at : PART + at + rows]
            return pltpu.make_async_copy(source, ref.at[at : at + rows], sem.at[index])

        return to

    @pl.when(core == 0)
    def _():
        leave_low(grads_keep).start()

    @pl.when(core == 1)
    def _():
        leave_low(grads_send).start()

    finish_norm(st[RS2], param(G2), 6)

    def hidden_back(m, parity, slot):
        t = c1_ref[m] - row(st.at[MU2], m)
        low = norm_grad(z_ref[m], t, m).astype(BF).astype(F32)
        total = row_sum(low)
        small[8:9, :] += total
        where = pl.ds(steps[base + m], 1)
        steps_grad[where, :] = steps_grad[where, :] + total
        put_shifted(e3[parity], slot, low, False)

    def centered(m):
        return load_x(m) - row(st.at[MU1], m)

    def first_back(m, parity, slot):
        both = conv(e3[parity], slot, k1t, True)
        for index in range(2):
            at = m + index
            g = both[index] * d1_ref[at].astype(F32)
            dn_ref[at] = g
            put_sums(at, g, g * (centered(at) * row(st.at[RS1], at)))

    overlapped(hidden_back, first_back)
    put_block(grads, 22, steps_grad[...])
    finish_norm(st[RS1], param(G1), 9)
    grads[BLOCKS * C : BLOCKS * C + 16, :] = small[...].astype(BF)
    away = pl.ds((1 - core) * HALF, HALF)

    def input_back(m):
        r_ref[m] = dr_ref[m] + norm_grad(dn_ref[m], centered(m), m)
        send_ref[m] = r_ref[m, away, :].astype(BF)

    for a in range(2):
        for index in range(3):
            input_back(3 * a + index)
        weight_taps(grads, 13, a, at_ref, e3)

    pieces = [leave_high(0, 7 * C, 14), leave_high(7 * C, PART - 7 * C, 15)]

    @pl.when(core == 0)
    def _():
        pieces[0](grads_send).start()

    @pl.when(core == 1)
    def _():
        pieces[0](grads_keep).start()

    input_back(6)
    input_back(7)
    give += [
        pltpu.make_async_copy(r_ref.at[:, pl.ds(core * HALF, HALF)], input_own.at[mine], sem.at[10]),
        pltpu.make_async_copy(send_ref, input_send, sem.at[11]),
    ]
    for copy in give[2:]:
        copy.start()
    weight_taps(grads, 13, 2, at_ref, e3)

    @pl.when(core == 0)
    def _():
        last = pieces[1](grads_send)
        last.start()
        leave_low(grads_keep).wait()
        pieces[0](grads_send).wait()
        last.wait()

    @pl.when(core == 1)
    def _():
        last = pieces[1](grads_keep)
        last.start()
        leave_low(grads_send).wait()
        pieces[0](grads_keep).wait()
        last.wait()

    for copy in give:
        copy.wait()


def shape(*dims, kind=F32):
    return jax.ShapeDtypeStruct(dims, kind)


SMEM = pl.BlockSpec(memory_space=pltpu.SMEM)
VMEM = pl.BlockSpec(memory_space=pltpu.VMEM)
ANY = pl.BlockSpec(memory_space=pl.ANY)
FULL = 60 * 1024 * 1024
ALL = 62 * 1024 * 1024
MOST = 40 * 1024 * 1024
LEAST = 16 * 1024 * 1024
HALF = POS // 2
MAP = (OWN, POS, C)
BANDS = (OWN, 2, HALF, C)
TRIPLE = (OWN // 2, PAD, 3 * C)
WIDE = (C, OWN * POS)
BLOCKS = 23
VECTORS = 11
PEERS = 64
EIGHT = 8
EIGHTH = 384
EVENLY = (1, 2, 4, 7, 3, 5, 6)
PART = EIGHT * EIGHTH
ROWS = 2 * PART


def run(place, steps, own_x, own_g, got, emb, dense, k1, k2, w_in, w_out, vectors):
    return pl.pallas_call(
        kernel_body,
        in_specs=[SMEM, SMEM] + [ANY] * 7 + [VMEM] * 13,
        out_specs=[ANY] * 6,
        out_shape=[
            shape(2 * OWN, HALF, C, kind=BF),
            shape(OWN, HALF, C, kind=BF),
            shape(2 * OWN, HALF, C),
            shape(OWN, HALF, C, kind=BF),
            shape(PART, C, kind=BF),
            shape(PART, C, kind=BF),
        ],
        scratch_shapes=[
            pltpu.VMEM(BANDS, BF),
            pltpu.VMEM(BANDS, BF),
            pltpu.VMEM(WIDE, BF),
            pltpu.VMEM(WIDE, BF),
            pltpu.VMEM(TRIPLE, BF),
            pltpu.VMEM(TRIPLE, BF),
            pltpu.VMEM(TRIPLE, BF),
            pltpu.VMEM(TRIPLE, BF),
            pltpu.VMEM(MAP, F32),
            pltpu.VMEM(MAP, BF),
            pltpu.VMEM(MAP, BF),
            pltpu.VMEM(MAP, F32),
            pltpu.VMEM(WIDE, BF),
            pltpu.VMEM(WIDE, BF),
            pltpu.VMEM((OWN, POS, 3 * C), BF),
            pltpu.VMEM(MAP, F32),
            pltpu.VMEM(MAP, F32),
            pltpu.VMEM(MAP, F32),
            pltpu.VMEM(BANDS, BF),
            pltpu.VMEM((OWN, HALF, C), BF),
            pltpu.VMEM((9 * C, C), BF),
            pltpu.VMEM((9 * C, C), BF),
            pltpu.VMEM((9 * C, C), BF),
            pltpu.VMEM((9 * C, C), BF),
            pltpu.VMEM((OWN, 8, 4 * C), F32),
            pltpu.VMEM((4 * C, C), BF),
            pltpu.VMEM((C, C), F32),
            pltpu.VMEM((ROWS, C), BF),
            pltpu.VMEM((16, C), F32),
            pltpu.VMEM((2, OWN, C), F32),
            pltpu.VMEM((4, OWN, C), F32),
            pltpu.VMEM((5, OWN, C), F32),
            pltpu.VMEM((OWN, C), F32),
            pltpu.VMEM((16, C), F32),
            pltpu.SemaphoreType.DMA((16 + OWN,)),
        ],
        compiler_params=pltpu.CompilerParams(vmem_limit_bytes=FULL),
        cost_estimate=pl.CostEstimate(
            flops=20 * 10**9, bytes_accessed=20 * 10**6, transcendentals=3 * 10**6
        ),
    )(place, steps, own_x, own_g, got, emb, dense, k1, k2, w_in, w_out, *vectors)


def swap(block):
    count = lax.axis_size("batch")
    return lax.ppermute(block, "batch", [(i, i ^ 1) for i in range(count)])


def join_body(place, mine_r, mine_i, got_r, got_i, out_r, out_i, wide_i, sem):
    there = pl.ds((1 - lax.rem(place[0], 2)) * OWN, OWN)
    first = pltpu.make_async_copy(got_r, out_r.at[there], sem.at[0])
    first.start()
    wide_i[...] = got_i[...].astype(F32)
    second = pltpu.make_async_copy(wide_i, out_i.at[there], sem.at[1])
    second.start()
    first.wait()
    second.wait()


def join(place, mine_r, mine_i, got_r, got_i):
    return pl.pallas_call(
        join_body,
        in_specs=[SMEM, ANY, ANY, VMEM, VMEM],
        out_specs=[ANY, ANY],
        out_shape=[shape(*mine_r.shape, kind=BF), shape(*mine_i.shape)],
        input_output_aliases={1: 0, 2: 1},
        scratch_shapes=[pltpu.VMEM((OWN, HALF, C), F32), pltpu.SemaphoreType.DMA((2,))],
        compiler_params=pltpu.CompilerParams(vmem_limit_bytes=LEAST),
        cost_estimate=pl.CostEstimate(flops=0, bytes_accessed=4 * 10**6, transcendentals=0),
    )(place, mine_r, mine_i, got_r, got_i)


def load_body(x, out, sem):
    copy = pltpu.make_async_copy(x, out, sem)
    copy.start()
    copy.wait()


def nearby(x):
    return pl.pallas_call(
        load_body,
        in_specs=[ANY],
        out_specs=VMEM,
        out_shape=shape(*x.shape, kind=x.dtype),
        scratch_shapes=[pltpu.SemaphoreType.DMA],
        compiler_params=pltpu.CompilerParams(vmem_limit_bytes=LEAST),
        cost_estimate=pl.CostEstimate(flops=0, bytes_accessed=2 * 10**6, transcendentals=0),
    )(x)


def wide(ref):
    return ref[...].astype(F32)


def eighth_of(index):
    return pl.ds(pl.multiple_of(index * EIGHTH, EIGHTH), EIGHTH)


def add_body(piece, mine, other, *outs):
    for mask in range(EIGHT):
        at = eighth_of(piece[0] ^ mask)
        total = mine[at, :].astype(F32) + other[at, :].astype(F32)
        outs[mask][...] = total.astype(BF)


def eight_body(*refs):
    total = wide(refs[0])
    for ref in refs[1:EIGHT]:
        total = total + wide(ref)
    low = total.astype(BF)
    for index, out in enumerate(refs[EIGHT:]):
        out[...] = low[index * (EIGHTH // 2) : (index + 1) * (EIGHTH // 2), :]


def two_body(mine, got, out):
    out[...] = (wide(mine) + wide(got)).astype(BF)


def last_body(mine_a, got_a, mine_b, got_b, out):
    out[0 : EIGHTH // 2, :] = (wide(mine_a) + wide(got_a)).astype(BF)
    out[EIGHTH // 2 :, :] = (wide(mine_b) + wide(got_b)).astype(BF)


def place_body(piece, *refs):
    for index, mask in enumerate((0,) + EVENLY):
        refs[EIGHT][eighth_of(piece[0] ^ mask), :] = refs[index][...]


def small_call(kernel, rows, count, *operands):
    scalars = [SMEM] if operands[0].ndim == 1 else []
    return pl.pallas_call(
        kernel,
        in_specs=scalars + [VMEM] * (len(operands) - len(scalars)),
        out_specs=[VMEM] * count,
        out_shape=[shape(rows, C, kind=BF)] * count,
        compiler_params=pltpu.CompilerParams(vmem_limit_bytes=LEAST),
        cost_estimate=pl.CostEstimate(flops=10**6, bytes_accessed=10**6, transcendentals=0),
    )(*operands)


def shifts(core):
    return [core, core, 1 - core]


def lines(index):
    return [
        (index // 2 // 4**axis + 3 * shift) % 4 for axis, shift in enumerate(shifts(index % 2))
    ]


def device_at(places, core):
    chip = sum(
        (place + shift) % 4 * 4**axis
        for axis, (place, shift) in enumerate(zip(places, shifts(core)))
    )
    return 2 * chip + core


def exchange(block, moved):
    pairs = [
        (index, device_at(moved(lines(index)), index % 2)) for index in range(2 * PEERS)
    ]
    return lax.ppermute(block, "batch", pairs)


def near(mask):
    return lambda places: [p ^ (mask >> axis & 1) for axis, p in enumerate(places)]


def far(axis):
    return lambda places: [3 - p if at == axis else p for at, p in enumerate(places)]


def all_sum(keep, other, device, meanwhile, afterwards):
    bits = [(place + 1) // 2 % 2 for place in lines(device)]
    piece = (bits[0] + 2 * bits[1] + 4 * bits[2]).reshape(1).astype(jnp.int32)
    keep, other = lax.optimization_barrier((nearby(keep), other))
    arrived = meanwhile(other)
    sends = small_call(add_body, EIGHTH, EIGHT, piece, keep, other)
    early, late = EVENLY[:3], EVENLY[3:]
    got = [exchange(sends[mask], near(mask)) for mask in early]
    held, arrived = lax.optimization_barrier(([sends[mask] for mask in late], arrived))
    got += [exchange(block, near(mask)) for block, mask in zip(held, late)]
    first, beside = lax.optimization_barrier((sends[0], afterwards(arrived)))
    a, b = small_call(eight_body, EIGHTH // 2, 2, first, *got)
    for step in range(2):
        a, b = (
            small_call(two_body, EIGHTH // 2, 1, part, exchange(part, far((step + first) % 3)))[0]
            for first, part in enumerate((a, b))
        )
    whole = small_call(
        last_body, EIGHTH, 1, a, exchange(a, far(2)), b, exchange(b, far(0))
    )[0]
    got = [exchange(whole, near(mask)) for mask in EVENLY]
    mine = small_call(place_body, PART, 1, piece, whole, *got)[0]
    return mine, swap(mine), beside


def write_half(high, part, emb, dense, outs, stage, wide_stage, table, emb_ref, dense_ref, sem):
    second_grad, in_grad, out_grad, first_grad, dense_grad, emb_grad = outs
    if high:
        places = [out_grad] + [first_grad.at[index] for index in range(9)]
        fetch = [
            pltpu.make_async_copy(emb, emb_ref, sem.at[18]),
            pltpu.make_async_copy(dense, dense_ref, sem.at[19]),
        ]
        for copy in fetch:
            copy.start()
    else:
        places = [second_grad.at[index] for index in range(9)]
        places += [in_grad.at[:, index * C : (index + 1) * C] for index in range(3)]
    copies = []

    def leave(source, to):
        copy = pltpu.make_async_copy(source, to, sem.at[len(copies)])
        copy.start()
        copies.append(copy)

    for index, to in enumerate(places):
        stage[index] = part[index * C : (index + 1) * C, :].astype(F32)
        leave(stage.at[index], to)
    if high:
        table[...] = part[10 * C : 11 * C, :]
        for copy in fetch:
            copy.wait()
        for index in range(4):
            columns = slice(index * C, (index + 1) * C)
            u = emb_ref[:, columns]
            s = logistic(u)
            active = u * s
            wide_stage[0, index] = mm(active.astype(BF).T, table[...])
            leave(wide_stage.at[0, index], dense_grad.at[columns, :])
            slope = s + active * (1.0 - s)
            wide_stage[1, index] = mm_nt(table[...], dense_ref[columns, :]) * slope
            leave(wide_stage.at[1, index], emb_grad.at[:, columns])
    for copy in copies:
        copy.wait()


def finish_own_body(place, mine, emb, dense, *refs):
    outs, scratch = refs[:6], refs[6:]
    for core in range(2):

        @pl.when(lax.rem(place[0], 2) == core)
        def _():
            write_half(core == 1, mine, emb, dense, outs, *scratch)


def finish_other_body(place, mine, other, emb, dense, *refs):
    outs, vectors, scratch = refs[6:12], refs[12 : 12 + VECTORS], refs[12 + VECTORS :]
    core = lax.rem(place[0], 2)
    at = slice(11 * C, 11 * C + 16)
    rows = jnp.where(core == 1, mine[at, :].astype(F32), other[at, :].astype(F32))
    for index, out in enumerate(vectors):
        out[...] = rows[index : index + 1, :].reshape(C)
    for this in range(2):

        @pl.when(core == this)
        def _():
            write_half(this == 0, other, emb, dense, outs, *scratch)


def finish(place, mine, other, emb, dense):
    dims = [(9, C, C), (C, 3 * C), (C, C), (9, C, C), (4 * C, C), (C, 4 * C)]
    settings = dict(
        scratch_shapes=[
            pltpu.VMEM((12, C, C), F32),
            pltpu.VMEM((2, 4, C, C), F32),
            pltpu.VMEM((C, C), BF),
            pltpu.VMEM((C, 4 * C), F32),
            pltpu.VMEM((4 * C, C), BF),
            pltpu.SemaphoreType.DMA((20,)),
        ],
        compiler_params=pltpu.CompilerParams(vmem_limit_bytes=LEAST),
        cost_estimate=pl.CostEstimate(
            flops=10**8, bytes_accessed=6 * 10**6, transcendentals=10**5
        ),
    )
    outs = pl.pallas_call(
        finish_own_body,
        in_specs=[SMEM, VMEM, ANY, ANY],
        out_specs=[ANY] * 6,
        out_shape=[shape(*d) for d in dims],
        **settings,
    )(place, mine, emb, dense)
    return pl.pallas_call(
        finish_other_body,
        in_specs=[SMEM, VMEM, VMEM, ANY, ANY] + [ANY] * 6,
        out_specs=[ANY] * 6 + [VMEM] * VECTORS,
        out_shape=[shape(*d) for d in dims] + [shape(C)] * VECTORS,
        input_output_aliases={5 + index: index for index in range(6)},
        **settings,
    )(place, mine, other, emb, dense, *outs)


def body(
    features, timesteps, embedding, first_gain, first_shift, first_kernel, first_bias, time_dense,
    second_gain, second_shift, second_kernel, second_bias, mixer_gain, mixer_shift, project_in,
    query_bias, value_bias, project_out, output_bias, cotangent,
):
    device = lax.axis_index("batch")
    own_x = features.reshape(2 * OWN, HALF, C)
    own_g = cotangent.reshape(2 * OWN, HALF, C)
    there = (1 - device % 2) * OWN
    place = device.reshape(1).astype(jnp.int32)
    got = swap(
        jnp.concatenate(
            [
                lax.dynamic_slice_in_dim(own_x, there, OWN),
                lax.dynamic_slice_in_dim(own_g, there, OWN),
            ]
        )
    )
    vectors = (
        first_gain, first_shift, first_bias, second_gain, second_shift, second_bias,
        mixer_gain, mixer_shift, query_bias, value_bias, output_bias,
    )
    result, result_send, input_grad, input_send, keep, send = run(
        place, timesteps, own_x, own_g, got, embedding, time_dense,
        first_kernel.reshape(9 * C, C), second_kernel.reshape(9 * C, C), project_in, project_out,
        vectors,
    )
    def swap_maps(block):
        first, second, _ = lax.optimization_barrier((result_send, input_send, block))
        return swap(first), swap(second)

    def join_maps(arrived):
        return join(place, result, input_grad, *arrived)

    mine, other, (result, input_grad) = all_sum(keep, swap(send), device, swap_maps, join_maps)
    (
        second_kernel_grad, in_grad, out_grad, first_kernel_grad, time_dense_grad, embedding_grad,
        *rows,
    ) = finish(place, mine, other, embedding, time_dense)
    banded = features.shape
    return (
        result.reshape(banded),
        input_grad.reshape(banded),
        embedding_grad,
        rows[9],
        rows[10],
        first_kernel_grad.reshape(3, 3, C, C),
        rows[8],
        time_dense_grad,
        rows[6],
        rows[7],
        second_kernel_grad.reshape(3, 3, C, C),
        rows[5],
        rows[3],
        rows[4],
        in_grad,
        rows[0],
        rows[1],
        out_grad,
        rows[2],
    )


def solution(mesh):
    split = P("batch", None, None, None, None)
    return jax.shard_map(
        body,
        mesh=mesh,
        in_specs=(split,) + (P(),) * 18 + (split,),
        out_specs=(split, split) + (P(),) * 17,
        check_vma=False,
    )
```
